1024 devices in a mesh: expert: 64 (over y, z_hi, x, core), replica: 16 (over z_lo).
Axes of the slice: x: 4, y: 4, z: 32 (z_hi: 2, z_lo: 16; z = z_hi * 16 + z_lo), core: 2. Of those that a mesh axis runs over, the one named last changes fastest.
Arguments:
- tokens: bfloat16 [65536, 1024], P(('expert', 'replica')), may hold values from -6 to 6
- route_ids: int32 [65536, 6], P(('expert', 'replica')), may hold values from 0 to 63, all different within a row; in each aligned block of 64 rows (0 to 63, 64 to 127, ...) at most 7 rows name the same one
- route_weights: bfloat16 [65536, 6], P(('expert', 'replica')), may hold values from 0.049804688 to 0.5
- out_grad: bfloat16 [65536, 1024], P(('expert', 'replica')), may hold values from -3 to 3
- w_gate: bfloat16 [64, 1024, 384], P('expert'), may hold values from -0.1875 to 0.1875
- w_up: bfloat16 [64, 1024, 384], P('expert'), may hold values from -0.1875 to 0.1875
- w_down: bfloat16 [64, 1024, 384], P('expert'), may hold values from -0.3125 to 0.3125
- mom_gate: float32 [64, 1024, 384], P('expert', 'replica'), may hold values from -6 to 6
- mom_up: float32 [64, 1024, 384], P('expert', 'replica'), may hold values from -6 to 6
- mom_down: float32 [64, 1024, 384], P('expert', 'replica'), may hold values from -6 to 6
Outputs:
- grad_tokens: bfloat16 [65536, 1024], P(('expert', 'replica'))
- grad_route: bfloat16 [65536, 6], P(('expert', 'replica'))
- new_gate: float32 [64, 1024, 384], P('expert', 'replica')
- new_up: float32 [64, 1024, 384], P('expert', 'replica')
- new_down: float32 [64, 1024, 384], P('expert', 'replica')
The draws below stay inside these ranges and needn't reach their ends.
Inputs may be any that keep to these rules, and one draw needn't show every extreme that they name: `route_ids`: each row names 6 different experts. Among the 64 rows of one device no expert is named more than 7 times, a bound that some block reaches.
All inputs are finite; a program needn't handle non-finite values.
Results may differ from the reference program's by a relative error of at most 0.015.
Values may be sent and summed in bfloat16 or wider, within the bound.
A program may use at most 32 MiB of HBM per device.

```python
import math
import jax
import jax.numpy as jnp
import numpy as np
from jax import lax

D = 1024
FF = 384
TOPK = 6
EXP_DEV = 1
TOK_DEV = 64
EXPERTS = 64
CAP = 7
TOKENS = 65536
N_EXPERT = 64
N_REPLICA = 16


def steps_of(own_key, extent, pieces, least, top_value):
    gain, own = 1.0, jax.random.fold_in(own_key, 6)
    for dim, blocks in pieces:
        draws = jnp.exp(jax.random.uniform(jax.random.fold_in(own, dim), (blocks,), jnp.float32, least / len(pieces), top_value / len(pieces)))
        gain = gain * jnp.repeat(draws, extent[dim] // blocks).reshape([-1 if axis == dim else 1 for axis in range(len(extent))])
    return gain


def deal_out(key, own, number, rows, count, top, limit, slope):
    ranking = jax.random.permutation(key, count)
    packed, usual = portions_of(count, rows * top, limit, slope, True), portions_of(count, rows * top, limit, slope, False)
    places = jnp.arange(count)

    def named(tallies, rotation):
        used = int((tallies > 0).sum())
        fixed = max(1, used // 4)
        moved = fixed + (places - fixed + rotation * (used - fixed)) % max(1, count - fixed)
        return jnp.zeros((count,), jnp.int32).at[ranking[jnp.where(places < fixed, places, moved)]].set(jnp.asarray(tallies, jnp.int32))

    tallies = jnp.where(number % 4 == 0, named(packed, number // 4), named(usual, number - number // 4 - 1))
    mixed = jax.random.permutation(jax.random.fold_in(own, 3), count)
    donor, receiver = mixed[0:count // 2 * 2:2], mixed[1:count // 2 * 2:2]
    margin = jnp.minimum(tallies[donor] - 1, limit - tallies[receiver]) // 2
    margin = jnp.where((donor == ranking[0]) | (receiver == ranking[0]) | (tallies[receiver] == 0), 0, jnp.maximum(margin, 0))
    moved = jax.random.randint(jax.random.fold_in(own, 4), (count // 2,), 0, 1 << 20) % (margin + 1)
    tallies = tallies.at[donor].add(-moved).at[receiver].add(moved)
    labels = jnp.searchsorted(jnp.cumsum(tallies), jnp.arange(rows * top), side="right").astype(jnp.int32)
    table = labels.reshape(top, rows).T
    table = table[jax.random.permutation(jax.random.fold_in(own, 1), rows)]
    rotation = jax.random.randint(jax.random.fold_in(own, 2), (rows, 1), 0, top)
    return jnp.take_along_axis(table, (jnp.arange(top)[None, :] + rotation) % top, axis=1)


def portions_of(amount, total, most, slope, full):
    weights = [(1 << 20) // math.isqrt(standing ** slope) + 1 for standing in range(1, amount + 1)]
    largest = most if full else min(most, max(-(-total // amount), total * weights[0] // sum(weights)))
    least = 1 if total - largest >= amount - 1 else 0
    given, surplus = [largest] + [least] * (amount - 1), total - largest - least * (amount - 1)
    while surplus > 0:
        movable = [i for i in range(1, amount) if given[i] < largest] or [i for i in range(1, amount) if given[i] < most]
        mass, budget = sum([weights[i] for i in movable]), surplus
        for i in movable:
            addition = min(most - given[i], max(1, budget * weights[i] // mass), surplus)
            given[i] = given[i] + addition
            surplus = surplus - addition
    return np.array(given)


def normal_values(stream_key, extent, width, bound, shards=(), kind=jnp.bfloat16):
    entries = width * jax.random.normal(stream_key, extent, jnp.float32)
    if shards:
        entries = entries * steps_of(stream_key, extent, shards, -0.22, 0.18)
    return jnp.clip(entries, -bound, bound).astype(kind)


def setup_inputs(seed: int = 0) -> dict:
    arg_keys = jax.random.split(jax.random.key(seed), 11)
    tokens = normal_values(arg_keys[0], (TOKENS, D), 1.0, 6.0, ((0, 1024),))
    route_ids_keys = jax.random.split(jax.random.fold_in(arg_keys[1], 1), TOKENS // TOK_DEV)
    route_ids_turns = jax.random.permutation(jax.random.fold_in(arg_keys[1], 3), TOKENS // TOK_DEV)
    route_ids = jax.vmap(lambda own, number: deal_out(jax.random.fold_in(arg_keys[1], 2), own, number, TOK_DEV, EXPERTS, TOPK, CAP, 2))(route_ids_keys, route_ids_turns).reshape((TOKENS, TOPK))
    route_weights = jnp.clip(jnp.exp(math.log(0.5) - 2.306499 * jax.random.uniform(arg_keys[2], (TOKENS, TOPK), jnp.float32) ** steps_of(arg_keys[2], (TOKENS, TOPK), ((0, 1024),), -0.2, 0.2)), 0.049804688, 0.5).astype(jnp.bfloat16)
    out_grad = normal_values(arg_keys[3], (TOKENS, D), 0.5, 3.0, ((0, 1024),))
    w_gate = normal_values(arg_keys[4], (EXPERTS, D, FF), D ** -0.5, 0.1875, ((0, 64),))
    w_up = normal_values(arg_keys[5], (EXPERTS, D, FF), D ** -0.5, 0.1875, ((0, 64),))
    w_down = normal_values(arg_keys[6], (EXPERTS, D, FF), FF ** -0.5, 0.3125, ((0, 64),))
    mom_gate = normal_values(arg_keys[7], (EXPERTS, D, FF), 1.0, 6.0, ((0, 64), (1, 16)), jnp.float32)
    mom_up = normal_values(arg_keys[8], (EXPERTS, D, FF), 1.0, 6.0, ((0, 64), (1, 16)), jnp.float32)
    mom_down = normal_values(arg_keys[9], (EXPERTS, D, FF), 1.0, 6.0, ((0, 64), (1, 16)), jnp.float32)
    return {"tokens": tokens, "route_ids": route_ids, "route_weights": route_weights, "out_grad": out_grad, "w_gate": w_gate, "w_up": w_up, "w_down": w_down, "mom_gate": mom_gate, "mom_up": mom_up, "mom_down": mom_down}


def slot_table(ids, experts, cap):
    flat = ids.reshape(-1)
    onehot = (flat[:, None] == jnp.arange(experts, dtype=jnp.int32)[None, :]).astype(jnp.int32)
    before = jnp.cumsum(onehot, axis=0) - onehot
    position = jnp.sum(before * onehot, axis=1).astype(jnp.int32)
    return flat * cap + position


def expert_step(args):
    rows, grads, weights, gate_w, up_w, down_w = args
    gate_act = jnp.dot(rows, gate_w, preferred_element_type=jnp.float32)
    up_act = jnp.dot(rows, up_w, preferred_element_type=jnp.float32)
    sig = 1.0 / (1.0 + jnp.exp(-gate_act))
    act = gate_act * sig
    hidden = act * up_act
    back = jnp.dot(grads, down_w, preferred_element_type=jnp.float32)
    route_grad = jnp.sum(hidden * back, axis=1).astype(jnp.bfloat16)
    scale = weights.astype(jnp.float32)[:, None]
    gh = scale * back
    grad_gate = (gh * up_act * sig * (1.0 + gate_act * (1.0 - sig))).astype(jnp.bfloat16)
    grad_up = (gh * act).astype(jnp.bfloat16)
    dims = (((1,), (1,)), ((), ()))
    slot_grad = lax.dot_general(grad_gate, gate_w, dims, preferred_element_type=jnp.float32)
    slot_grad = (slot_grad + lax.dot_general(grad_up, up_w, dims, preferred_element_type=jnp.float32)).astype(jnp.bfloat16)
    scaled = (scale * grads.astype(jnp.float32)).astype(jnp.bfloat16)
    hidden_b = hidden.astype(jnp.bfloat16)
    rdims = (((0,), (0,)), ((), ()))
    part_gate = lax.dot_general(rows, grad_gate, rdims, preferred_element_type=jnp.float32)
    part_up = lax.dot_general(rows, grad_up, rdims, preferred_element_type=jnp.float32)
    part_down = lax.dot_general(scaled, hidden_b, rdims, preferred_element_type=jnp.float32)
    return slot_grad, route_grad, jnp.concatenate([part_gate, part_up, part_down], axis=1)


def reference(tokens, route_ids, route_weights, out_grad, w_gate, w_up, w_down, mom_gate, mom_up, mom_down):
    experts = EXP_DEV * N_EXPERT
    cap = (7 * TOK_DEV * TOPK) // (6 * experts)
    depth = N_EXPERT * cap
    routes = TOK_DEV * TOPK

    def blocks(array):
        return array.reshape((N_EXPERT, N_REPLICA, TOK_DEV) + array.shape[1:])

    tok_blocks = blocks(tokens)
    id_blocks = blocks(route_ids)
    weight_blocks = blocks(route_weights)
    grad_blocks = blocks(out_grad)
    token_of = jnp.arange(routes, dtype=jnp.int32) // TOPK
    total = jnp.zeros((experts, D, 3 * FF), jnp.float32)
    tok_list = []
    route_list = []
    for replica_index in range(N_REPLICA):
        ids = id_blocks[:, replica_index]
        slots = jax.vmap(lambda item: slot_table(item, experts, cap))(ids)
        expert_of = ids.reshape(N_EXPERT, routes).astype(jnp.int32)
        position = slots - expert_of * cap
        row_of = (jnp.arange(N_EXPERT, dtype=jnp.int32)[:, None] * cap + position).astype(jnp.int32)
        rows = tok_blocks[:, replica_index][:, token_of]
        grads = grad_blocks[:, replica_index][:, token_of]
        weights = weight_blocks[:, replica_index].reshape(N_EXPERT, routes)
        buf_rows = jnp.zeros((experts, depth, D), tokens.dtype).at[expert_of, row_of].set(rows)
        buf_grads = jnp.zeros((experts, depth, D), out_grad.dtype).at[expert_of, row_of].set(grads)
        buf_weights = jnp.zeros((experts, depth), route_weights.dtype).at[expert_of, row_of].set(weights)
        slot_grad, route_grad, parts = lax.map(expert_step, (buf_rows, buf_grads, buf_weights, w_gate, w_up, w_down))
        rounded = lax.optimization_barrier(parts.astype(jnp.bfloat16))
        total = total + rounded.astype(jnp.float32)
        picked = slot_grad[expert_of, row_of].reshape(N_EXPERT, TOK_DEV, TOPK, D)
        tok_list.append(jnp.sum(picked.astype(jnp.float32), axis=2).astype(jnp.bfloat16))
        route_list.append(route_grad[expert_of, row_of].reshape(N_EXPERT, TOK_DEV, TOPK))
    grad_tokens = jnp.stack(tok_list, axis=1).reshape(N_EXPERT * N_REPLICA * TOK_DEV, D)
    grad_route = jnp.stack(route_list, axis=1).reshape(N_EXPERT * N_REPLICA * TOK_DEV, TOPK)
    new_gate = 0.9 * mom_gate + 0.1 * total[:, :, :FF]
    new_up = 0.9 * mom_up + 0.1 * total[:, :, FF:2 * FF]
    new_down = 0.9 * mom_down + 0.1 * total[:, :, 2 * FF:]
    return grad_tokens, grad_route, new_gate, new_up, new_down
```

```python
import functools

import jax
import jax.numpy as jnp
from jax import lax
from jax.experimental import pallas as pl
from jax.experimental.pallas import tpu as pltpu
from jax.sharding import PartitionSpec as P

MESH = pl.DeviceIdType.MESH
F32 = jnp.float32
BF16 = jnp.bfloat16
CAP = 7
BLOCKS = 8

NN = (((1,), (0,)), ((), ()))
NT = (((1,), (1,)), ((), ()))
TN = (((0,), (0,)), ((), ()))


def dot(a, b, dims=NN):
    return lax.dot_general(a, b, dims, preferred_element_type=F32)


def iota(shape, dim):
    return lax.broadcasted_iota(jnp.int32, shape, dim)


def kernel(
    inner, replicas, topk,
    tok, ids, rw, og, wg, wu, wd, mg, mu, md,
    out_tok, out_route, out_g, out_u, out_d,
    snd, rcv, bsnd, brcv, pw, part, from_left, from_right,
    xs, gs, sc, gate, up, back, gg, gu, hid, slot, table,
    dsend, drecv, rsend, rrecv, wsend, wrecv, lsend, lrecv, gsend, grecv,
):
    tokens_here, width = tok.shape
    units = wg.shape[2]
    peers = rcv.shape[1] // 16
    experts = 2 * peers
    shard = width // replicas
    half_rows = width // 2
    wblock = half_rows // BLOCKS

    e = lax.axis_index("expert")
    r = lax.axis_index("replica")
    half = (e // inner) % 2
    me = (e // (2 * inner)) * inner + e % inner
    flip = inner * (1 - 2 * half)
    at_last = (r + 1) // replicas
    at_first = 1 - (r + replicas - 1) // replicas
    right = (e + at_last * flip, (r + 1) % replicas)
    left = (e + at_first * flip, (r + replicas - 1) % replicas)

    def peer(g):
        return ((g // inner) * 2 * inner + half * inner + g % inner, r)

    def ahead(i):
        return (me + i) % peers

    barrier = pltpu.get_barrier_semaphore()

    @pl.loop(1, peers)
    def _(i):
        pl.semaphore_signal(barrier, inc=1, device_id=peer(ahead(i)), device_id_type=MESH)

    for side in (left, right):
        pl.semaphore_signal(barrier, inc=1, device_id=side, device_id_type=MESH)

    eye = (iota((tokens_here, tokens_here), 0) == iota((tokens_here, tokens_here), 1)).astype(BF16)
    ids_t = dot(ids[...].astype(F32).astype(BF16), eye, TN)
    rw_t = dot(rw[...], eye, TN)
    row = iota((experts, 1), 0)
    group = row % peers
    order = (
        (group // inner) * 2 * inner + ((row // peers + half) % 2) * inner + group % inner
    ).astype(F32)
    named = jnp.zeros((experts, tokens_here), F32)
    weight_of = jnp.zeros((experts, tokens_here), F32)
    for k in range(topk):
        hit = ids_t[k : k + 1, :] == order
        named = jnp.where(hit, 1.0, named)
        weight_of = jnp.where(hit, rw_t[k : k + 1, :], weight_of)
    earlier = (iota((tokens_here, tokens_here), 0) < iota((tokens_here, tokens_here), 1)).astype(BF16)
    posm = jnp.where(named > 0.0, dot(named.astype(BF16), earlier), -1.0)
    table[...] = posm
    lane = iota((experts, 128), 1)
    slot_weight = jnp.zeros((experts, 128), F32)
    for j in range(CAP):
        w = jnp.sum(jnp.where(posm == float(j), weight_of, 0.0), axis=1, keepdims=True)
        slot_weight = jnp.where(lane == j, w, slot_weight)
    posm_b = posm.astype(BF16)
    slot_weight = slot_weight.astype(BF16)

    rows16 = 16 * peers
    rr = iota((rows16, experts), 0)
    ee = iota((rows16, experts), 1)
    pick_row = iota((rows16, 1), 0)
    for h in range(2):
        repeat = (ee == h * peers + rr // 16).astype(BF16)
        spread = dot(repeat, posm_b)
        chosen = spread == (pick_row % 8).astype(F32)
        upper = pick_row % 16 < 8
        from_tok = jnp.where(jnp.logical_and(chosen, upper), 1.0, 0.0).astype(BF16)
        from_og = jnp.where(jnp.logical_and(chosen, jnp.logical_not(upper)), 1.0, 0.0).astype(BF16)
        weights = jnp.where(pick_row % 16 == 7, dot(repeat, slot_weight), 0.0)
        step = width // 4 if width >= 512 else width // 2
        for c in range(0, width, step):
            block = dot(from_tok, tok[:, c : c + step]) + dot(from_og, og[:, c : c + step])
            if c == 0:
                snd[h, :, 0:128] = (block[:, 0:128] + weights).astype(BF16)
                snd[h, :, 128:step] = block[:, 128:].astype(BF16)
            else:
                snd[h, :, c : c + step] = block.astype(BF16)

    pl.semaphore_wait(barrier, peers + 1)

    def rows_of(g):
        return pl.ds(pl.multiple_of(g * 16, 16), 16)

    def dispatch(h, g, source):
        return pltpu.make_async_remote_copy(
            src_ref=snd.at[h, rows_of(g)],
            dst_ref=rcv.at[h, rows_of(source)],
            send_sem=dsend.at[h, g],
            recv_sem=drecv.at[h, source],
            device_id=peer(g),
            device_id_type=MESH,
        )

    def send_back(g, source):
        return pltpu.make_async_remote_copy(
            src_ref=bsnd.at[rows_of(g)],
            dst_ref=brcv.at[rows_of(source)],
            send_sem=rsend.at[g],
            recv_sem=rrecv.at[source],
            device_id=peer(g),
            device_id_type=MESH,
        )

    def weight_copy(d, m, b, source):
        rows = pl.ds(pl.multiple_of(d * half_rows + b * wblock, wblock), wblock)
        return pltpu.make_async_remote_copy(
            src_ref=source.at[0, rows] if source is not pw else pw.at[m, rows],
            dst_ref=pw.at[m, rows],
            send_sem=wsend.at[d, m * BLOCKS + b],
            recv_sem=wrecv.at[d, m * BLOCKS + b],
            device_id=right if d == 0 else left,
            device_id_type=MESH,
        )

    own = (wg, wu, wd)

    def pass_weights(m):
        @pl.loop(0, BLOCKS)
        def _(b):
            for d, edge in ((0, at_last), (1, at_first)):

                @pl.when(edge == 0)
                def _():
                    copy = weight_copy(d, m, b, pw)
                    copy.wait_recv()
                    copy.start()

    for m in range(3):
        for d, edge in ((0, at_last), (1, at_first)):

            @pl.when(edge == 1)
            def _():
                @pl.loop(0, BLOCKS)
                def _(b):
                    weight_copy(d, m, b, own[m]).start()

    for h in range(2):

        @pl.loop(1, peers)
        def _(i):
            dispatch(h, ahead(i), me).start()

        rcv[h, rows_of(me)] = snd[h, rows_of(me)]

    def expert(h, gate_w, up_w, down_w):
        @pl.loop(1, peers)
        def _(i):
            dispatch(h, me, ahead(i)).wait_recv()

        groups = min(4, peers)
        count = groups * 8

        @pl.loop(0, peers // groups)
        def _(i):
            block = rcv[h, pl.ds(pl.multiple_of(i * groups * 16, 16), groups * 16), :]
            block = block.astype(F32).reshape(groups, 2, 8, width)
            x, g = block[:, 0], block[:, 1]
            spread = jnp.broadcast_to(x[:, 7:8, 0:128], (groups, 8, 128)).reshape(count, 128)
            own_lane = iota((count, 128), 1) == iota((count, 128), 0) % 8
            own_lane = jnp.logical_and(own_lane, iota((count, 128), 1) < CAP)
            scale = jnp.sum(jnp.where(own_lane, spread, 0.0), axis=1, keepdims=True)
            x = x.reshape(count, width)
            g = g.reshape(count, width)
            x = jnp.where(iota((count, 1), 0) % 8 == 7, 0.0, x)
            at = pl.ds(pl.multiple_of(i * count, count), count)
            xs[at] = x.astype(BF16)
            gs[at] = g.astype(BF16)
            sc[at] = (scale * g).astype(BF16)
            slot[h, at, 0:128] = jnp.broadcast_to(scale, (count, 128))

        gate[...] = dot(xs[...], gate_w[...])
        up[...] = dot(xs[...], up_w[...])
        back[...] = dot(gs[...], down_w[...])

        @pl.loop(0, peers // groups)
        def _(i):
            at = pl.ds(pl.multiple_of(i * count, count), count)
            scale = slot[h, at, 0:128][:, 0:1]
            a, u, b = gate[at], up[at], back[at]
            sig = 1.0 / (1.0 + jnp.exp(-a))
            act = a * sig
            hidden = act * u
            route = jnp.sum(hidden * b, axis=1, keepdims=True)
            gh = scale * b
            gg[h, at] = (gh * u * sig * (1.0 + a * (1.0 - sig))).astype(BF16)
            gu[h, at] = (gh * act).astype(BF16)
            hid[at] = hidden.astype(BF16)
            slot[h, at, 128:256] = jnp.broadcast_to(route, (count, 128))

        depth = min(256, width)

        @pl.loop(0, width // depth)
        def _(i):
            at = pl.ds(pl.multiple_of(i * depth, depth), depth)
            x = xs[:, at]
            part[h, 0, at] = dot(x, gg[h], TN).astype(BF16)
            part[h, 1, at] = dot(x, gu[h], TN).astype(BF16)
            part[h, 2, at] = dot(sc[:, at], hid[...], TN).astype(BF16)

    def token_grads(h, gate_w, up_w):
        count = 8 * peers
        route = slot[h, :, 128:256]
        own_lane = iota((count, 128), 1) == iota((count, 128), 0) % 8
        own_lane = jnp.logical_and(own_lane, iota((count, 128), 1) < CAP)
        route = jnp.where(own_lane, route, 0.0).reshape(peers, 8, 128)
        route = jnp.broadcast_to(jnp.sum(route, axis=1, keepdims=True), (peers, 8, 128))
        route = jnp.where(iota((count, 128), 0) % 8 == 7, route.reshape(count, 128), 0.0)
        slot[h] = dot(gg[h], gate_w[...], NT) + dot(gu[h], up_w[...], NT)
        slot[h, :, 0:128] += route

    pass_weights(0)
    expert(0, wg.at[0], wu.at[0], wd.at[0])
    pass_weights(1)
    pass_weights(2)
    for m in range(3):
        for d, edge in ((0, at_last), (1, at_first)):

            @pl.when(edge == 1)
            def _():
                @pl.loop(0, BLOCKS)
                def _(b):
                    weight_copy(d, m, b, pw).wait_recv()

    expert(1, pw.at[0], pw.at[1], pw.at[2])

    z = half * replicas + r

    def shard_of(k):
        owner = (z + k) % (2 * replicas)
        rows = pl.ds(pl.multiple_of((owner % replicas) * shard, shard), shard)
        return (owner // replicas + half) % 2, rows

    def to_right(s, m, source):
        return pltpu.make_async_remote_copy(
            src_ref=source,
            dst_ref=from_left.at[s, m],
            send_sem=lsend.at[s * 3 + m],
            recv_sem=lrecv.at[s * 3 + m],
            device_id=right,
            device_id_type=MESH,
        )

    def to_left(s, m, source):
        return pltpu.make_async_remote_copy(
            src_ref=source,
            dst_ref=from_right.at[s, m],
            send_sem=gsend.at[s * 3 + m],
            recv_sem=grecv.at[s * 3 + m],
            device_id=left,
            device_id_type=MESH,
        )

    h_r, rows_r = shard_of(replicas)
    h_l, rows_l = shard_of(replicas + 1)
    for m in range(3):
        to_right(0, m, part.at[h_r, m, rows_r]).start()
        to_left(0, m, part.at[h_l, m, rows_l]).start()

    token_grads(0, wg.at[0], wu.at[0])
    token_grads(1, pw.at[0], pw.at[1])
    groups = min(4, peers)

    @pl.loop(0, peers // groups)
    def _(i):
        at = pl.ds(pl.multiple_of(i * groups * 8, groups * 8), groups * 8)
        a = slot[0, at].reshape(groups, 1, 8, width)
        b = slot[1, at].reshape(groups, 1, 8, width)
        both = jnp.concatenate([a, b], axis=1).reshape(groups * 16, width)
        bsnd[pl.ds(pl.multiple_of(i * groups * 16, 16), groups * 16)] = both.astype(BF16)

    @pl.loop(1, peers)
    def _(i):
        send_back(ahead(i), me).start()

    brcv[rows_of(me)] = bsnd[rows_of(me)]

    def add_right(s, m):
        h, rows = shard_of(replicas - 1 - s)
        to_right(s, m, from_left.at[s, m]).wait_recv()
        total = from_left[s, m].astype(F32) + part[h, m, rows].astype(F32)
        from_left[s, m] = total.astype(BF16)
        to_right(s + 1, m, from_left.at[s, m]).start()

    def add_left(s, m):
        h, rows = shard_of(replicas + 2 + s)
        to_left(s, m, from_right.at[s, m]).wait_recv()
        total = from_right[s, m].astype(F32) + part[h, m, rows].astype(F32)
        from_right[s, m] = total.astype(BF16)
        to_left(s + 1, m, from_right.at[s, m]).start()

    def ring(lo, hi):
        @pl.loop(lo, hi)
        def _(s):
            for m in range(3):
                add_right(s, m)
                add_left(s, m)

    middle = (replicas - 2) // 2
    ring(0, middle)

    @pl.loop(1, peers)
    def _(i):
        send_back(me, ahead(i)).wait_recv()

    posm = table[...]
    take = (ee == ((rr // 8) % 2) * peers + rr // 16).astype(BF16)
    chosen = dot(take, posm.astype(BF16)) == (pick_row % 8).astype(F32)
    chosen = jnp.where(chosen, 1.0, 0.0).astype(BF16)
    step = min(256, width)
    for c in range(0, width, step):
        out_tok[:, c : c + step] = dot(chosen, brcv[:, c : c + step], TN).astype(BF16)
    se = iota((experts, rows16), 0)
    sr = iota((experts, rows16), 1)
    last_row = (sr == (se % peers) * 16 + (se // peers) * 8 + 7).astype(BF16)
    routes = dot(last_row, brcv[:, 0:128])
    value = jnp.zeros((experts, tokens_here), F32)
    for j in range(CAP):
        value = jnp.where(posm == float(j), routes[:, j : j + 1], value)
    ids_t = dot(ids[...].astype(F32).astype(BF16), eye, TN)
    by_k = jnp.zeros((8, tokens_here), F32)
    for k in range(topk):
        mine = jnp.sum(jnp.where(ids_t[k : k + 1, :] == order, value, 0.0), axis=0, keepdims=True)
        by_k = jnp.where(iota((8, tokens_here), 0) == k, mine, by_k)
    out_route[...] = dot(eye, by_k.astype(BF16), NT)[:, 0:topk].astype(BF16)

    ring(middle, replicas - 2)
    for m in range(3):
        add_right(replicas - 2, m)
    h, rows = shard_of(0)
    for m, (mom, out) in enumerate(((mg, out_g), (mu, out_u), (md, out_d))):
        to_left(replicas - 2, m, from_right.at[replicas - 2, m]).wait_recv()
        to_right(replicas - 1, m, from_left.at[replicas - 1, m]).wait_recv()
        total = part[h, m, rows].astype(F32) + from_right[replicas - 2, m].astype(F32)
        total = total + from_left[replicas - 1, m].astype(F32)
        out[0] = 0.9 * mom[0] + 0.1 * total

    for h in range(2):

        @pl.loop(1, peers)
        def _(i):
            dispatch(h, ahead(i), me).wait_send()

    @pl.loop(1, peers)
    def _(i):
        send_back(ahead(i), me).wait_send()

    for m in range(3):

        @pl.loop(0, BLOCKS)
        def _(b):
            for d in range(2):
                weight_copy(d, m, b, pw).wait_send()

        @pl.loop(0, replicas)
        def _(s):
            to_right(s, m, from_left.at[s, m]).wait_send()

        @pl.loop(0, replicas - 1)
        def _(s):
            to_left(s, m, from_right.at[s, m]).wait_send()


def per_device(
    tokens, route_ids, route_weights, out_grad, w_gate, w_up, w_down, mom_gate, mom_up, mom_down
):
    groups = lax.axis_size("expert")
    replicas = lax.axis_size("replica")
    peers = groups // 2
    inner = 8 if groups == 64 else peers
    tok_rows, width = tokens.shape
    units = w_gate.shape[2]
    shard = width // replicas
    topk = route_ids.shape[1]
    deep = 8 * peers
    vmem = pltpu.VMEM
    dma = pltpu.SemaphoreType.DMA
    return pl.pallas_call(
        functools.partial(kernel, inner, replicas, topk),
        out_shape=(
            jax.ShapeDtypeStruct(tokens.shape, BF16),
            jax.ShapeDtypeStruct(route_ids.shape, BF16),
            jax.ShapeDtypeStruct(mom_gate.shape, F32),
            jax.ShapeDtypeStruct(mom_up.shape, F32),
            jax.ShapeDtypeStruct(mom_down.shape, F32),
        ),
        in_specs=[pl.BlockSpec(memory_space=vmem)] * 10,
        out_specs=[pl.BlockSpec(memory_space=vmem)] * 5,
        scratch_shapes=[
            vmem((2, 16 * peers, width), BF16),
            vmem((2, 16 * peers, width), BF16),
            vmem((16 * peers, width), BF16),
            vmem((16 * peers, width), BF16),
            vmem((3, width, units), BF16),
            vmem((2, 3, width, units), BF16),
            vmem((replicas, 3, shard, units), BF16),
            vmem((replicas - 1, 3, shard, units), BF16),
            vmem((deep, width), BF16),
            vmem((deep, width), BF16),
            vmem((deep, width), BF16),
            vmem((deep, units), F32),
            vmem((deep, units), F32),
            vmem((deep, units), F32),
            vmem((2, deep, units), BF16),
            vmem((2, deep, units), BF16),
            vmem((deep, units), BF16),
            vmem((2, deep, width), F32),
            vmem((groups, tok_rows), F32),
            dma((2, peers)),
            dma((2, peers)),
            dma((peers,)),
            dma((peers,)),
            dma((2, 3 * BLOCKS)),
            dma((2, 3 * BLOCKS)),
            dma((3 * replicas,)),
            dma((3 * replicas,)),
            dma((3 * (replicas - 1),)),
            dma((3 * (replicas - 1),)),
        ],
        compiler_params=pltpu.CompilerParams(
            collective_id=0, has_side_effects=True, vmem_limit_bytes=56 * 1024 * 1024
        ),
        cost_estimate=pl.CostEstimate(
            flops=2 * 2 * deep * width * units * 8, bytes_accessed=8 * 2**20, transcendentals=2 * deep * units
        ),
    )(tokens, route_ids, route_weights, out_grad, w_gate, w_up, w_down, mom_gate, mom_up, mom_down)


def solution(mesh):
    both = P(("expert", "replica"), None)
    held = P("expert", None, None)
    split = P("expert", "replica", None)
    return jax.shard_map(
        per_device,
        mesh=mesh,
        in_specs=(both,) * 4 + (held,) * 3 + (split,) * 3,
        out_specs=(both, both, split, split, split),
        check_vma=False,
    )
```

```python
import functools

import jax
import jax.numpy as jnp
from jax import lax
from jax.experimental import pallas as pl
from jax.experimental.pallas import tpu as pltpu
from jax.sharding import PartitionSpec as P

MESH = pl.DeviceIdType.MESH
F32 = jnp.float32
BF16 = jnp.bfloat16
CAP = 7
BLOCKS = 32
NEAR = 64
LAG = 6
OWN_AT = 50

NN = (((1,), (0,)), ((), ()))
NT = (((1,), (1,)), ((), ()))
TN = (((0,), (0,)), ((), ()))


def dot(a, b, dims=NN):
    return lax.dot_general(a, b, dims, preferred_element_type=F32)


def iota(shape, dim):
    return lax.broadcasted_iota(jnp.int32, shape, dim)


def kernel(
    inner, replicas, topk,
    tok, ids, rw, og, wg, wu, wd, mg, mu, md,
    out_tok, out_route, out_g, out_u, out_d,
    snd, rcv, bsnd, brcv, pw, part, from_left, from_right,
    xs, gs, sc, gate, up, back, gg, gu, hid, slot, table,
    dsend, drecv, rsend, rrecv, wsend, wrecv, lsend, lrecv, gsend, grecv,
):
    tokens_here, width = tok.shape
    units = wg.shape[2]
    peers = rcv.shape[1] // 16
    experts = 2 * peers
    shard = width // replicas
    wblock = width // BLOCKS
    far = 3 * BLOCKS - NEAR

    e = lax.axis_index("expert")
    r = lax.axis_index("replica")
    half = (e // inner) % 2
    me = (e // (2 * inner)) * inner + e % inner
    flip = inner * (1 - 2 * half)
    at_last = (r + 1) // replicas
    at_first = 1 - (r + replicas - 1) // replicas
    right = (e + at_last * flip, (r + 1) % replicas)
    left = (e + at_first * flip, (r + replicas - 1) % replicas)

    def peer(g):
        return ((g // inner) * 2 * inner + half * inner + g % inner, r)

    def ahead(i):
        return (me + i) % peers

    barrier = pltpu.get_barrier_semaphore()

    @pl.loop(1, peers)
    def _(i):
        pl.semaphore_signal(barrier, inc=1, device_id=peer(ahead(i)), device_id_type=MESH)

    for side in (left, right):
        pl.semaphore_signal(barrier, inc=1, device_id=side, device_id_type=MESH)

    def rows_of(g):
        return pl.ds(pl.multiple_of(g * 16, 16), 16)

    def dispatch(h, g, source):
        return pltpu.make_async_remote_copy(
            src_ref=snd.at[h, rows_of(g)],
            dst_ref=rcv.at[h, rows_of(source)],
            send_sem=dsend.at[h, g],
            recv_sem=drecv.at[h, source],
            device_id=peer(g),
            device_id_type=MESH,
        )

    def send_back(g, source):
        return pltpu.make_async_remote_copy(
            src_ref=bsnd.at[rows_of(g)],
            dst_ref=brcv.at[rows_of(source)],
            send_sem=rsend.at[g],
            recv_sem=rrecv.at[source],
            device_id=peer(g),
            device_id_type=MESH,
        )

    def weight_copy(d, c, source):
        q = c if d == 0 else 3 * BLOCKS - 1 - c
        rows = pl.ds(pl.multiple_of((q % BLOCKS) * wblock, wblock), wblock)
        landing = pw.at[q // BLOCKS, rows]
        return pltpu.make_async_remote_copy(
            src_ref=landing if source is None else source.at[0, rows],
            dst_ref=landing,
            send_sem=wsend.at[d, c],
            recv_sem=wrecv.at[d, c],
            device_id=right if d == 0 else left,
            device_id_type=MESH,
        )

    place = (r, replicas - 1 - r)

    def comes(d, c):
        return jnp.logical_and(c >= 0, c < jnp.where(place[d] < replicas // 2, NEAR, far))

    def goes_on(d, c):
        sent = jnp.where(place[d] < replicas // 2 - 1, NEAR, jnp.where(place[d] < replicas - 1, far, 0))
        return jnp.logical_and(c >= 0, c < sent)

    def start_weights():
        for d in range(2):

            @pl.when(place[d] == replicas - 1)
            def _():
                for m, source in enumerate((wg, wu, wd)):
                    first, last = m * BLOCKS, (m + 1) * BLOCKS
                    if d == 1:
                        first, last = 3 * BLOCKS - last, 3 * BLOCKS - first
                    if first < NEAR:

                        @pl.loop(first, min(last, NEAR))
                        def _(c):
                            weight_copy(d, c, source).start()

    ticks = max(NEAR + LAG * (replicas // 2 - 1), far + LAG * (replicas - 1))

    def pass_weights(lo, hi):
        @pl.loop(lo, hi)
        def _(t):
            for d in range(2):
                c = t - LAG * place[d]

                @pl.when(comes(d, c))
                def _():
                    weight_copy(d, c, None).wait_recv()

                @pl.when(goes_on(d, c))
                def _():
                    weight_copy(d, c, None).start()

    pl.semaphore_wait(barrier, peers + 1)
    start_weights()

    eye = (iota((tokens_here, tokens_here), 0) == iota((tokens_here, tokens_here), 1)).astype(BF16)
    ids_t = dot(ids[...].astype(F32).astype(BF16), eye, TN)
    rw_t = dot(rw[...], eye, TN)
    row = iota((experts, 1), 0)
    group = row % peers
    order = (
        (group // inner) * 2 * inner + ((row // peers + half) % 2) * inner + group % inner
    ).astype(F32)
    named = jnp.zeros((experts, tokens_here), F32)
    weight_of = jnp.zeros((experts, tokens_here), F32)
    for k in range(topk):
        hit = ids_t[k : k + 1, :] == order
        named = jnp.where(hit, 1.0, named)
        weight_of = jnp.where(hit, rw_t[k : k + 1, :], weight_of)
    earlier = (iota((tokens_here, tokens_here), 0) < iota((tokens_here, tokens_here), 1)).astype(BF16)
    posm = jnp.where(named > 0.0, dot(named.astype(BF16), earlier), -1.0)
    table[...] = posm
    lane = iota((experts, 128), 1)
    slot_weight = jnp.zeros((experts, 128), F32)
    for j in range(CAP):
        w = jnp.sum(jnp.where(posm == float(j), weight_of, 0.0), axis=1, keepdims=True)
        slot_weight = jnp.where(lane == j, w, slot_weight)
    posm_b = posm.astype(BF16)
    slot_weight = slot_weight.astype(BF16)

    rows16 = 16 * peers
    rr = iota((rows16, experts), 0)
    ee = iota((rows16, experts), 1)
    pick_row = iota((rows16, 1), 0)
    for h in range(2):
        repeat = (ee == h * peers + rr // 16).astype(BF16)
        spread = dot(repeat, posm_b)
        chosen = spread == (pick_row % 8).astype(F32)
        upper = pick_row % 16 < 8
        from_tok = jnp.where(jnp.logical_and(chosen, upper), 1.0, 0.0).astype(BF16)
        from_og = jnp.where(jnp.logical_and(chosen, jnp.logical_not(upper)), 1.0, 0.0).astype(BF16)
        weights = jnp.where(pick_row % 16 == 7, dot(repeat, slot_weight), 0.0)
        step = width // 4 if width >= 512 else width // 2
        for c in range(0, width, step):
            block = dot(from_tok, tok[:, c : c + step]) + dot(from_og, og[:, c : c + step])
            if c == 0:
                snd[h, :, 0:128] = (block[:, 0:128] + weights).astype(BF16)
                snd[h, :, 128:step] = block[:, 128:].astype(BF16)
            else:
                snd[h, :, c : c + step] = block.astype(BF16)

    for h in range(2):

        @pl.loop(1, peers)
        def _(i):
            dispatch(h, ahead(i), me).start()

        rcv[h, rows_of(me)] = snd[h, rows_of(me)]

    def expert(h, gate_w, up_w, down_w):
        @pl.loop(1, peers)
        def _(i):
            dispatch(h, me, ahead(i)).wait_recv()

        groups = min(4, peers)
        count = groups * 8

        @pl.loop(0, peers // groups)
        def _(i):
            block = rcv[h, pl.ds(pl.multiple_of(i * groups * 16, 16), groups * 16), :]
            block = block.astype(F32).reshape(groups, 2, 8, width)
            x, g = block[:, 0], block[:, 1]
            spread = jnp.broadcast_to(x[:, 7:8, 0:128], (groups, 8, 128)).reshape(count, 128)
            own_lane = iota((count, 128), 1) == iota((count, 128), 0) % 8
            own_lane = jnp.logical_and(own_lane, iota((count, 128), 1) < CAP)
            scale = jnp.sum(jnp.where(own_lane, spread, 0.0), axis=1, keepdims=True)
            x = x.reshape(count, width)
            g = g.reshape(count, width)
            x = jnp.where(iota((count, 1), 0) % 8 == 7, 0.0, x)
            at = pl.ds(pl.multiple_of(i * count, count), count)
            xs[at] = x.astype(BF16)
            gs[at] = g.astype(BF16)
            sc[at] = (scale * g).astype(BF16)
            slot[h, at, 0:128] = jnp.broadcast_to(scale, (count, 128))

        gate[...] = dot(xs[...], gate_w[...])
        up[...] = dot(xs[...], up_w[...])
        back[...] = dot(gs[...], down_w[...])

        @pl.loop(0, peers // groups)
        def _(i):
            at = pl.ds(pl.multiple_of(i * count, count), count)
            scale = slot[h, at, 0:128][:, 0:1]
            a, u, b = gate[at], up[at], back[at]
            sig = 1.0 / (1.0 + jnp.exp(-a))
            act = a * sig
            hidden = act * u
            route = jnp.sum(hidden * b, axis=1, keepdims=True)
            gh = scale * b
            gg[h, at] = (gh * u * sig * (1.0 + a * (1.0 - sig))).astype(BF16)
            gu[h, at] = (gh * act).astype(BF16)
            hid[at] = hidden.astype(BF16)
            slot[h, at, 128:256] = jnp.broadcast_to(route, (count, 128))

        depth = min(256, width)

        @pl.loop(0, width // depth)
        def _(i):
            at = pl.ds(pl.multiple_of(i * depth, depth), depth)
            x = xs[:, at]
            part[h, 0, at] = dot(x, gg[h], TN).astype(BF16)
            part[h, 1, at] = dot(x, gu[h], TN).astype(BF16)
            part[h, 2, at] = dot(sc[:, at], hid[...], TN).astype(BF16)

    def token_grads(h, gate_w, up_w):
        count = 8 * peers
        route = slot[h, :, 128:256]
        own_lane = iota((count, 128), 1) == iota((count, 128), 0) % 8
        own_lane = jnp.logical_and(own_lane, iota((count, 128), 1) < CAP)
        route = jnp.where(own_lane, route, 0.0).reshape(peers, 8, 128)
        route = jnp.broadcast_to(jnp.sum(route, axis=1, keepdims=True), (peers, 8, 128))
        route = jnp.where(iota((count, 128), 0) % 8 == 7, route.reshape(count, 128), 0.0)
        slot[h] = dot(gg[h], gate_w[...], NT) + dot(gu[h], up_w[...], NT)
        slot[h, :, 0:128] += route

    pass_weights(0, min(OWN_AT, ticks))
    expert(0, wg.at[0], wu.at[0], wd.at[0])
    pass_weights(min(OWN_AT, ticks), ticks)
    expert(1, pw.at[0], pw.at[1], pw.at[2])

    z = half * replicas + r

    def shard_of(k):
        owner = (z + k) % (2 * replicas)
        rows = pl.ds(pl.multiple_of((owner % replicas) * shard, shard), shard)
        return (owner // replicas + half) % 2, rows

    def to_right(s, m, source):
        return pltpu.make_async_remote_copy(
            src_ref=source,
            dst_ref=from_left.at[s, m],
            send_sem=lsend.at[s * 3 + m],
            recv_sem=lrecv.at[s * 3 + m],
            device_id=right,
            device_id_type=MESH,
        )

    def to_left(s, m, source):
        return pltpu.make_async_remote_copy(
            src_ref=source,
            dst_ref=from_right.at[s, m],
            send_sem=gsend.at[s * 3 + m],
            recv_sem=grecv.at[s * 3 + m],
            device_id=left,
            device_id_type=MESH,
        )

    h_r, rows_r = shard_of(replicas)
    h_l, rows_l = shard_of(replicas + 1)
    for m in range(3):
        to_right(0, m, part.at[h_r, m, rows_r]).start()
        to_left(0, m, part.at[h_l, m, rows_l]).start()

    token_grads(0, wg.at[0], wu.at[0])
    token_grads(1, pw.at[0], pw.at[1])
    groups = min(4, peers)

    @pl.loop(0, peers // groups)
    def _(i):
        at = pl.ds(pl.multiple_of(i * groups * 8, groups * 8), groups * 8)
        a = slot[0, at].reshape(groups, 1, 8, width)
        b = slot[1, at].reshape(groups, 1, 8, width)
        both = jnp.concatenate([a, b], axis=1).reshape(groups * 16, width)
        bsnd[pl.ds(pl.multiple_of(i * groups * 16, 16), groups * 16)] = both.astype(BF16)

    @pl.loop(1, peers)
    def _(i):
        send_back(ahead(i), me).start()

    brcv[rows_of(me)] = bsnd[rows_of(me)]

    def add_right(s, m):
        h, rows = shard_of(replicas - 1 - s)
        to_right(s, m, from_left.at[s, m]).wait_recv()
        total = from_left[s, m].astype(F32) + part[h, m, rows].astype(F32)
        from_left[s, m] = total.astype(BF16)
        to_right(s + 1, m, from_left.at[s, m]).start()

    def add_left(s, m):
        h, rows = shard_of(replicas + 2 + s)
        to_left(s, m, from_right.at[s, m]).wait_recv()
        total = from_right[s, m].astype(F32) + part[h, m, rows].astype(F32)
        from_right[s, m] = total.astype(BF16)
        to_left(s + 1, m, from_right.at[s, m]).start()

    def ring(lo, hi):
        @pl.loop(lo, hi)
        def _(s):
            for m in range(3):
                add_right(s, m)
                add_left(s, m)

    middle = (replicas - 2) // 2
    ring(0, middle)

    @pl.loop(1, peers)
    def _(i):
        send_back(me, ahead(i)).wait_recv()

    posm = table[...]
    take = (ee == ((rr // 8) % 2) * peers + rr // 16).astype(BF16)
    chosen = dot(take, posm.astype(BF16)) == (pick_row % 8).astype(F32)
    chosen = jnp.where(chosen, 1.0, 0.0).astype(BF16)
    step = min(256, width)
    for c in range(0, width, step):
        out_tok[:, c : c + step] = dot(chosen, brcv[:, c : c + step], TN).astype(BF16)
    se = iota((experts, rows16), 0)
    sr = iota((experts, rows16), 1)
    last_row = (sr == (se % peers) * 16 + (se // peers) * 8 + 7).astype(BF16)
    routes = dot(last_row, brcv[:, 0:128])
    value = jnp.zeros((experts, tokens_here), F32)
    for j in range(CAP):
        value = jnp.where(posm == float(j), routes[:, j : j + 1], value)
    ids_t = dot(ids[...].astype(F32).astype(BF16), eye, TN)
    by_k = jnp.zeros((8, tokens_here), F32)
    for k in range(topk):
        mine = jnp.sum(jnp.where(ids_t[k : k + 1, :] == order, value, 0.0), axis=0, keepdims=True)
        by_k = jnp.where(iota((8, tokens_here), 0) == k, mine, by_k)
    out_route[...] = dot(eye, by_k.astype(BF16), NT)[:, 0:topk].astype(BF16)

    ring(middle, replicas - 2)
    for m in range(3):
        add_right(replicas - 2, m)
    h, rows = shard_of(0)
    for m, (mom, out) in enumerate(((mg, out_g), (mu, out_u), (md, out_d))):
        to_left(replicas - 2, m, from_right.at[replicas - 2, m]).wait_recv()
        to_right(replicas - 1, m, from_left.at[replicas - 1, m]).wait_recv()
        total = part[h, m, rows].astype(F32) + from_right[replicas - 2, m].astype(F32)
        total = total + from_left[replicas - 1, m].astype(F32)
        out[0] = 0.9 * mom[0] + 0.1 * total

    for h in range(2):

        @pl.loop(1, peers)
        def _(i):
            dispatch(h, ahead(i), me).wait_send()

    @pl.loop(1, peers)
    def _(i):
        send_back(ahead(i), me).wait_send()

    @pl.loop(0, NEAR)
    def _(c):
        for d in range(2):

            @pl.when(jnp.logical_or(place[d] == replicas - 1, goes_on(d, c)))
            def _():
                weight_copy(d, c, None).wait_send()

    for m in range(3):

        @pl.loop(0, replicas)
        def _(s):
            to_right(s, m, from_left.at[s, m]).wait_send()

        @pl.loop(0, replicas - 1)
        def _(s):
            to_left(s, m, from_right.at[s, m]).wait_send()


def per_device(
    tokens, route_ids, route_weights, out_grad, w_gate, w_up, w_down, mom_gate, mom_up, mom_down
):
    groups = lax.axis_size("expert")
    replicas = lax.axis_size("replica")
    peers = groups // 2
    inner = 8 if groups == 64 else peers
    tok_rows, width = tokens.shape
    units = w_gate.shape[2]
    shard = width // replicas
    topk = route_ids.shape[1]
    deep = 8 * peers
    vmem = pltpu.VMEM
    dma = pltpu.SemaphoreType.DMA
    return pl.pallas_call(
        functools.partial(kernel, inner, replicas, topk),
        out_shape=(
            jax.ShapeDtypeStruct(tokens.shape, BF16),
            jax.ShapeDtypeStruct(route_ids.shape, BF16),
            jax.ShapeDtypeStruct(mom_gate.shape, F32),
            jax.ShapeDtypeStruct(mom_up.shape, F32),
            jax.ShapeDtypeStruct(mom_down.shape, F32),
        ),
        in_specs=[pl.BlockSpec(memory_space=vmem)] * 10,
        out_specs=[pl.BlockSpec(memory_space=vmem)] * 5,
        scratch_shapes=[
            vmem((2, 16 * peers, width), BF16),
            vmem((2, 16 * peers, width), BF16),
            vmem((16 * peers, width), BF16),
            vmem((16 * peers, width), BF16),
            vmem((3, width, units), BF16),
            vmem((2, 3, width, units), BF16),
            vmem((replicas, 3, shard, units), BF16),
            vmem((replicas - 1, 3, shard, units), BF16),
            vmem((deep, width), BF16),
            vmem((deep, width), BF16),
            vmem((deep, width), BF16),
            vmem((deep, units), F32),
            vmem((deep, units), F32),
            vmem((deep, units), F32),
            vmem((2, deep, units), BF16),
            vmem((2, deep, units), BF16),
            vmem((deep, units), BF16),
            vmem((2, deep, width), F32),
            vmem((groups, tok_rows), F32),
            dma((2, peers)),
            dma((2, peers)),
            dma((peers,)),
            dma((peers,)),
            dma((2, NEAR)),
            dma((2, NEAR)),
            dma((3 * replicas,)),
            dma((3 * replicas,)),
            dma((3 * (replicas - 1),)),
            dma((3 * (replicas - 1),)),
        ],
        compiler_params=pltpu.CompilerParams(
            collective_id=0, has_side_effects=True, vmem_limit_bytes=56 * 1024 * 1024
        ),
        cost_estimate=pl.CostEstimate(
            flops=2 * 2 * deep * width * units * 8, bytes_accessed=8 * 2**20, transcendentals=2 * deep * units
        ),
    )(tokens, route_ids, route_weights, out_grad, w_gate, w_up, w_down, mom_gate, mom_up, mom_down)


def solution(mesh):
    both = P(("expert", "replica"), None)
    held = P("expert", None, None)
    split = P("expert", "replica", None)
    return jax.shard_map(
        per_device,
        mesh=mesh,
        in_specs=(both,) * 4 + (held,) * 3 + (split,) * 3,
        out_specs=(both, both, split, split, split),
        check_vma=False,
    )
```

```python
import functools

import jax
import jax.numpy as jnp
from jax import lax
from jax.experimental import pallas as pl
from jax.experimental.pallas import tpu as pltpu
from jax.sharding import PartitionSpec as P

MESH = pl.DeviceIdType.MESH
F32 = jnp.float32
BF16 = jnp.bfloat16
CAP = 7
BLOCKS = 32
LAG = 6
PIECES = 6
OWN_AT = 28
RETURNED_AT = 9

NN = (((1,), (0,)), ((), ()))
NT = (((1,), (1,)), ((), ()))
TN = (((0,), (0,)), ((), ()))


def dot(a, b, dims=NN):
    return lax.dot_general(a, b, dims, preferred_element_type=F32)


def iota(shape, dim):
    return lax.broadcasted_iota(jnp.int32, shape, dim)


def kernel(
    inner, replicas, topk,
    tok, ids, rw, og, wg, wu, wd, mg, mu, md,
    out_tok, out_route, out_g, out_u, out_d,
    snd, rcv, bsnd, brcv, pw, part, from_left, from_right,
    xs, gs, sc, gate, up, back, gg, gu, hid, scales, routes, slot, table,
    dsend, drecv, rsend, rrecv, wsend, wrecv, lsend, lrecv, gsend, grecv,
):
    tokens_here, width = tok.shape
    units = wg.shape[2]
    peers = rcv.shape[1] // 16
    experts = 2 * peers
    shard = width // replicas
    wblock = width // BLOCKS
    groups = min(4, peers)
    count = groups * 8
    deep = 8 * peers
    quarters = 4 if peers >= 32 else 1

    e = lax.axis_index("expert")
    r = lax.axis_index("replica")
    half = (e // inner) % 2
    me = (e // (2 * inner)) * inner + e % inner
    flip = inner * (1 - 2 * half)
    at_last = (r + 1) // replicas
    at_first = 1 - (r + replicas - 1) // replicas
    right = (e + at_last * flip, (r + 1) % replicas)
    left = (e + at_first * flip, (r + replicas - 1) % replicas)

    def peer(g):
        return ((g // inner) * 2 * inner + half * inner + g % inner, r)

    def ahead(i):
        return (me + i) % peers

    barrier = pltpu.get_barrier_semaphore()

    @pl.loop(1, peers)
    def _(i):
        pl.semaphore_signal(barrier, inc=1, device_id=peer(ahead(i)), device_id_type=MESH)

    for side in (left, right):
        pl.semaphore_signal(barrier, inc=1, device_id=side, device_id_type=MESH)

    def rows_of(g):
        return pl.ds(pl.multiple_of(g * 16, 16), 16)

    def dispatch(h, g, source):
        return pltpu.make_async_remote_copy(
            src_ref=snd.at[h, rows_of(g)],
            dst_ref=rcv.at[h, rows_of(source)],
            send_sem=dsend.at[h, g],
            recv_sem=drecv.at[h, source],
            device_id=peer(g),
            device_id_type=MESH,
        )

    def send_back(g, source):
        return pltpu.make_async_remote_copy(
            src_ref=bsnd.at[rows_of(g)],
            dst_ref=brcv.at[rows_of(source)],
            send_sem=rsend.at[g],
            recv_sem=rrecv.at[source],
            device_id=peer(g),
            device_id_type=MESH,
        )

    def weight_copy(d, c, source):
        q = c if d == 0 else 3 * BLOCKS - 1 - c
        rows = pl.ds(pl.multiple_of((q % BLOCKS) * wblock, wblock), wblock)
        landing = pw.at[q // BLOCKS, rows]
        return pltpu.make_async_remote_copy(
            src_ref=landing if source is None else source.at[0, rows],
            dst_ref=landing,
            send_sem=wsend.at[d, c],
            recv_sem=wrecv.at[d, c],
            device_id=right if d == 0 else left,
            device_id_type=MESH,
        )

    place = (r, replicas - 1 - r)

    def reach(p):
        return 3 * BLOCKS // 2 + (replicas - 1 - 2 * p) * (LAG // 2)

    def comes(d, c):
        return jnp.logical_and(c >= 0, c < reach(place[d]))

    def goes_on(d, c):
        more = jnp.logical_and(place[d] < replicas - 1, c < reach(place[d] + 1))
        return jnp.logical_and(c >= 0, more)

    def start_weights():
        for d in range(2):

            @pl.when(place[d] == replicas - 1)
            def _():
                for m, source in enumerate((wg, wu, wd)):
                    first, last = m * BLOCKS, (m + 1) * BLOCKS
                    if d == 1:
                        first, last = 3 * BLOCKS - last, 3 * BLOCKS - first
                    if first < reach(0):

                        @pl.loop(first, min(last, reach(0)))
                        def _(c):
                            weight_copy(d, c, source).start()

    ticks = reach(0)

    def pass_weights(lo, hi, work=None):
        @pl.loop(lo, hi)
        def _(t):
            for d in range(2):
                c = t - LAG * place[d]

                @pl.when(comes(d, c))
                def _():
                    weight_copy(d, c, None).wait_recv()

                @pl.when(goes_on(d, c))
                def _():
                    weight_copy(d, c, None).start()

            if work is not None:
                work(t - lo)

    pl.semaphore_wait(barrier, peers + 1)
    start_weights()

    ids_t = ids[...].astype(F32)
    rw_t = rw[...].astype(F32)
    row = iota((experts, 1), 0)
    group = row % peers
    order = (
        (group // inner) * 2 * inner + ((row // peers + half) % 2) * inner + group % inner
    ).astype(F32)
    named = jnp.zeros((experts, tokens_here), F32)
    weight_of = jnp.zeros((experts, tokens_here), F32)
    for k in range(topk):
        hit = ids_t[k : k + 1, :] == order
        named = jnp.where(hit, 1.0, named)
        weight_of = jnp.where(hit, rw_t[k : k + 1, :], weight_of)
    earlier = (iota((tokens_here, tokens_here), 0) < iota((tokens_here, tokens_here), 1)).astype(BF16)
    posm = jnp.where(named > 0.0, dot(named.astype(BF16), earlier), -1.0)
    table[...] = posm
    lane = iota((experts, 128), 1)
    slot_weight = jnp.zeros((experts, 128), F32)
    for j in range(CAP):
        w = jnp.sum(jnp.where(posm == float(j), weight_of, 0.0), axis=1, keepdims=True)
        slot_weight = jnp.where(lane == j, w, slot_weight)
    posm_b = posm.astype(BF16)
    slot_weight = slot_weight.astype(BF16)

    rows16 = 16 * peers
    rr = iota((rows16, experts), 0)
    ee = iota((rows16, experts), 1)
    pick_row = iota((rows16, 1), 0)
    for h in range(2):
        repeat = (ee == h * peers + rr // 16).astype(BF16)
        spread = dot(repeat, posm_b)
        chosen = spread == (pick_row % 8).astype(F32)
        upper = pick_row % 16 < 8
        from_tok = jnp.where(jnp.logical_and(chosen, upper), 1.0, 0.0).astype(BF16)
        from_og = jnp.where(jnp.logical_and(chosen, jnp.logical_not(upper)), 1.0, 0.0).astype(BF16)
        weights = jnp.where(pick_row % 16 == 7, dot(repeat, slot_weight), 0.0)
        step = width // 4 if width >= 512 else width // 2
        for c in range(0, width, step):
            tick = h * (width // step) + c // step
            pass_weights(tick, tick + 1)
            block = dot(from_tok, tok[:, c : c + step]) + dot(from_og, og[:, c : c + step])
            if c == 0:
                snd[h, :, 0:128] = (block[:, 0:128] + weights).astype(BF16)
                snd[h, :, 128:step] = block[:, 128:].astype(BF16)
            else:
                snd[h, :, c : c + step] = block.astype(BF16)

        @pl.loop(1, peers)
        def _(i):
            dispatch(h, ahead(i), me).start()

        rcv[h, rows_of(me)] = snd[h, rows_of(me)]


    def received(h):
        @pl.loop(1, peers)
        def _(i):
            dispatch(h, me, ahead(i)).wait_recv()

    def unpack(h):
        def some(i):
            block = rcv[h, pl.ds(pl.multiple_of(i * groups * 16, 16), groups * 16), :]
            block = block.astype(F32).reshape(groups, 2, 8, width)
            x, g = block[:, 0], block[:, 1]
            spread = jnp.broadcast_to(x[:, 7:8, 0:128], (groups, 8, 128)).reshape(count, 128)
            own_lane = iota((count, 128), 1) == iota((count, 128), 0) % 8
            own_lane = jnp.logical_and(own_lane, iota((count, 128), 1) < CAP)
            scale = jnp.sum(jnp.where(own_lane, spread, 0.0), axis=1, keepdims=True)
            x = x.reshape(count, width)
            g = g.reshape(count, width)
            x = jnp.where(iota((count, 1), 0) % 8 == 7, 0.0, x)
            at = pl.ds(pl.multiple_of(i * count, count), count)
            xs[h, at] = x.astype(BF16)
            gs[h, at] = g.astype(BF16)
            sc[h, at] = (scale * g).astype(BF16)
            scales[h, at] = jnp.broadcast_to(scale, (count, 128))

        return some

    def expert(h, gate_w, up_w, down_w):
        def gates(i):
            gate[...] = dot(xs[h], gate_w[...])

        def ups(i):
            up[...] = dot(xs[h], up_w[...])

        def backs(i):
            back[...] = dot(gs[h], down_w[...])

        def products(i):
            at = pl.ds(pl.multiple_of(i * count, count), count)
            scale = scales[h, at][:, 0:1]
            a, u, b = gate[at], up[at], back[at]
            sig = 1.0 / (1.0 + jnp.exp(-a))
            act = a * sig
            hidden = act * u
            route = jnp.sum(hidden * b, axis=1, keepdims=True)
            gh = scale * b
            gg[h, at] = (gh * u * sig * (1.0 + a * (1.0 - sig))).astype(BF16)
            gu[h, at] = (gh * act).astype(BF16)
            hid[at] = hidden.astype(BF16)
            routes[h, at] = jnp.broadcast_to(route, (count, 128))

        depth = min(256, width)

        def parts(i):
            at = pl.ds(pl.multiple_of(i * depth, depth), depth)
            x = xs[h, :, at]
            part[h, 0, at] = dot(x, gg[h], TN).astype(BF16)
            part[h, 1, at] = dot(x, gu[h], TN).astype(BF16)
            part[h, 2, at] = dot(sc[h, :, at], hid[...], TN).astype(BF16)

        turns, blocks = peers // groups, width // depth
        return ((gates, 1), (ups, 1), (backs, 1), (products, turns), (parts, blocks))

    def token_grads(h, at, rows, gate_w, up_w):
        own_lane = iota((rows, 128), 1) == iota((rows, 128), 0) % 8
        own_lane = jnp.logical_and(own_lane, iota((rows, 128), 1) < CAP)
        route = jnp.where(own_lane, routes[h, at], 0.0).reshape(rows // 8, 8, 128)
        route = jnp.broadcast_to(jnp.sum(route, axis=1, keepdims=True), (rows // 8, 8, 128))
        route = jnp.where(iota((rows, 128), 0) % 8 == 7, route.reshape(rows, 128), 0.0)
        slot[h, at] = dot(gg[h, at], gate_w[...], NT) + dot(gu[h, at], up_w[...], NT)
        slot[h, at, 0:128] += route

    def own_quarter(i):
        rows = deep // quarters
        at = pl.ds(pl.multiple_of(i * rows, rows), rows)
        token_grads(0, at, rows, wg.at[0], wu.at[0])

    turns = peers // groups
    tick = 2 * (width // step)
    pass_weights(tick, OWN_AT)
    tick = OWN_AT
    received(0)
    stages = ((unpack(0), turns),) + expert(0, wg.at[0], wu.at[0], wd.at[0]) + ((own_quarter, quarters),)
    for work, times in stages:
        pass_weights(tick, tick + times, work)
        tick += times
    received(1)
    pass_weights(tick, tick + turns, unpack(1))
    pass_weights(tick + turns, max(ticks, tick + turns))
    for work, times in expert(1, pw.at[0], pw.at[1], pw.at[2]):
        pl.loop(0, times)(work)

    z = half * replicas + r

    def shard_of(k, m):
        owner = (z + k) % (2 * replicas)
        piece = 3 * shard // PIECES
        first = (owner % replicas) * shard + (m % (PIECES // 3)) * piece
        rows = pl.ds(pl.multiple_of(first, piece), piece)
        return (owner // replicas + half) % 2, m // (PIECES // 3), rows

    def to_right(s, m, source):
        return pltpu.make_async_remote_copy(
            src_ref=source,
            dst_ref=from_left.at[s, m],
            send_sem=lsend.at[s * PIECES + m],
            recv_sem=lrecv.at[s * PIECES + m],
            device_id=right,
            device_id_type=MESH,
        )

    def to_left(s, m, source):
        return pltpu.make_async_remote_copy(
            src_ref=source,
            dst_ref=from_right.at[s, m],
            send_sem=gsend.at[s * PIECES + m],
            recv_sem=grecv.at[s * PIECES + m],
            device_id=left,
            device_id_type=MESH,
        )

    for m in range(PIECES):
        to_right(0, m, part.at[shard_of(replicas, m)]).start()
        to_left(0, m, part.at[shard_of(replicas + 1, m)]).start()

    def return_some(i):
        rows = deep // quarters
        quarter = (me * quarters // peers + i) % quarters
        at = pl.ds(pl.multiple_of(quarter * rows, rows), rows)
        token_grads(1, at, rows, pw.at[0], pw.at[1])
        a = slot[0, at].reshape(rows // 8, 1, 8, width)
        b = slot[1, at].reshape(rows // 8, 1, 8, width)
        blocks = jnp.concatenate([a, b], axis=1).reshape(rows * 2, width)
        bsnd[pl.ds(pl.multiple_of(quarter * rows * 2, rows * 2), rows * 2)] = blocks.astype(BF16)
        some = peers // quarters

        @pl.loop(0, some)
        def _(j):
            g = quarter * some + (me + j) % some

            @pl.when(g != me)
            def _():
                send_back(g, me).start()

            @pl.when(g == me)
            def _():
                brcv[rows_of(me)] = bsnd[rows_of(me)]

    def add_right(s, m):
        h, w, rows = shard_of(replicas - 1 - s, m)
        to_right(s, m, from_left.at[s, m]).wait_recv()
        total = from_left[s, m].astype(F32) + part[h, w, rows].astype(F32)
        from_left[s, m] = total.astype(BF16)
        to_right(s + 1, m, from_left.at[s, m]).start()

    def add_left(s, m):
        h, w, rows = shard_of(replicas + 2 + s, m)
        to_left(s, m, from_right.at[s, m]).wait_recv()
        total = from_right[s, m].astype(F32) + part[h, w, rows].astype(F32)
        from_right[s, m] = total.astype(BF16)
        to_left(s + 1, m, from_right.at[s, m]).start()

    def ring(lo, hi, work=None):
        @pl.loop(min(lo, replicas - 2), min(hi, replicas - 2))
        def _(s):
            for m in range(PIECES):
                add_right(s, m)
                add_left(s, m)
            if work is not None:
                work(s - lo)

    ring(0, quarters, return_some)
    ring(quarters, RETURNED_AT)

    @pl.loop(1, peers)
    def _(i):
        send_back(me, ahead(i)).wait_recv()

    posm = table[...]
    take = (ee == ((rr // 8) % 2) * peers + rr // 16).astype(BF16)
    chosen = dot(take, posm.astype(BF16)) == (pick_row % 8).astype(F32)
    chosen = jnp.where(chosen, 1.0, 0.0).astype(BF16)
    step = min(256, width)
    for c in range(0, width, step):
        out_tok[:, c : c + step] = dot(chosen, brcv[:, c : c + step], TN).astype(BF16)
    ring(RETURNED_AT, RETURNED_AT + 1)
    se = iota((experts, rows16), 0)
    sr = iota((experts, rows16), 1)
    last_row = (sr == (se % peers) * 16 + (se // peers) * 8 + 7).astype(BF16)
    returned = dot(last_row, brcv[:, 0:128])
    value = jnp.zeros((experts, tokens_here), F32)
    for j in range(CAP):
        value = jnp.where(posm == float(j), returned[:, j : j + 1], value)
    ids_t = ids[...].astype(F32)
    by_k = jnp.zeros((8, tokens_here), F32)
    for k in range(topk):
        mine = jnp.sum(jnp.where(ids_t[k : k + 1, :] == order, value, 0.0), axis=0, keepdims=True)
        by_k = jnp.where(iota((8, tokens_here), 0) == k, mine, by_k)
    out_route[...] = by_k[0:topk].astype(BF16)

    ring(RETURNED_AT + 1, replicas - 2)
    for m in range(PIECES):
        add_right(replicas - 2, m)
    piece = 3 * shard // PIECES
    moms, outs = (mg, mu, md), (out_g, out_u, out_d)
    for m in range(PIECES):
        h, w, rows = shard_of(0, m)
        to_left(replicas - 2, m, from_right.at[replicas - 2, m]).wait_recv()
        to_right(replicas - 1, m, from_left.at[replicas - 1, m]).wait_recv()
        total = part[h, w, rows].astype(F32) + from_right[replicas - 2, m].astype(F32)
        total = total + from_left[replicas - 1, m].astype(F32)
        at = pl.ds((m % (PIECES // 3)) * piece, piece)
        outs[w][0, at] = 0.9 * moms[w][0, at] + 0.1 * total

    for h in range(2):

        @pl.loop(1, peers)
        def _(i):
            dispatch(h, ahead(i), me).wait_send()

    @pl.loop(1, peers)
    def _(i):
        send_back(ahead(i), me).wait_send()

    @pl.loop(0, ticks)
    def _(c):
        for d in range(2):

            @pl.when(jnp.logical_or(place[d] == replicas - 1, goes_on(d, c)))
            def _():
                weight_copy(d, c, None).wait_send()

    for m in range(PIECES):

        @pl.loop(0, replicas)
        def _(s):
            to_right(s, m, from_left.at[s, m]).wait_send()

        @pl.loop(0, replicas - 1)
        def _(s):
            to_left(s, m, from_right.at[s, m]).wait_send()


def per_device(
    tokens, route_ids, route_weights, out_grad, w_gate, w_up, w_down, mom_gate, mom_up, mom_down
):
    groups = lax.axis_size("expert")
    replicas = lax.axis_size("replica")
    peers = groups // 2
    inner = 8 if groups == 64 else peers
    tok_rows, width = tokens.shape
    units = w_gate.shape[2]
    shard = width // replicas
    topk = route_ids.shape[1]
    deep = 8 * peers
    vmem = pltpu.VMEM
    dma = pltpu.SemaphoreType.DMA
    outs = pl.pallas_call(
        functools.partial(kernel, inner, replicas, topk),
        out_shape=(
            jax.ShapeDtypeStruct(tokens.shape, BF16),
            jax.ShapeDtypeStruct((topk, tok_rows), BF16),
            jax.ShapeDtypeStruct(mom_gate.shape, F32),
            jax.ShapeDtypeStruct(mom_up.shape, F32),
            jax.ShapeDtypeStruct(mom_down.shape, F32),
        ),
        in_specs=[pl.BlockSpec(memory_space=vmem)] * 10,
        out_specs=[pl.BlockSpec(memory_space=vmem)] * 5,
        scratch_shapes=[
            vmem((2, 16 * peers, width), BF16),
            vmem((2, 16 * peers, width), BF16),
            vmem((16 * peers, width), BF16),
            vmem((16 * peers, width), BF16),
            vmem((3, width, units), BF16),
            vmem((2, 3, width, units), BF16),
            vmem((replicas, PIECES, 3 * shard // PIECES, units), BF16),
            vmem((replicas - 1, PIECES, 3 * shard // PIECES, units), BF16),
            vmem((2, deep, width), BF16),
            vmem((2, deep, width), BF16),
            vmem((2, deep, width), BF16),
            vmem((deep, units), F32),
            vmem((deep, units), F32),
            vmem((deep, units), F32),
            vmem((2, deep, units), BF16),
            vmem((2, deep, units), BF16),
            vmem((deep, units), BF16),
            vmem((2, deep, 128), F32),
            vmem((2, deep, 128), F32),
            vmem((2, deep, width), F32),
            vmem((groups, tok_rows), F32),
            dma((2, peers)),
            dma((2, peers)),
            dma((peers,)),
            dma((peers,)),
            dma((2, 3 * BLOCKS)),
            dma((2, 3 * BLOCKS)),
            dma((PIECES * replicas,)),
            dma((PIECES * replicas,)),
            dma((PIECES * (replicas - 1),)),
            dma((PIECES * (replicas - 1),)),
        ],
        compiler_params=pltpu.CompilerParams(
            collective_id=0, has_side_effects=True, vmem_limit_bytes=56 * 1024 * 1024
        ),
        cost_estimate=pl.CostEstimate(
            flops=2 * 2 * deep * width * units * 8, bytes_accessed=8 * 2**20, transcendentals=2 * deep * units
        ),
    )(tokens, route_ids.T, route_weights.T, out_grad, w_gate, w_up, w_down, mom_gate, mom_up, mom_down)
    return (outs[0], outs[1].T, *outs[2:])


def solution(mesh):
    both = P(("expert", "replica"), None)
    held = P("expert", None, None)
    split = P("expert", "replica", None)
    return jax.shard_map(
        per_device,
        mesh=mesh,
        in_specs=(both,) * 4 + (held,) * 3 + (split,) * 3,
        out_specs=(both, both, split, split, split),
        check_vma=False,
    )
```
